32 devices in a mesh: dp: 16 (over z, y, x), tensor: 2 (over core).
Axes of the slice: x: 2, y: 2, z: 4, core: 2. Of those that a mesh axis runs over, the one named last changes fastest.
Arguments:
- hidden_in: bfloat16 [512, 8192], P(None, 'tensor'), may hold values from -6 to 6
- teacher: bfloat16 [512, 8192], P(None, 'tensor'), may hold values from -3 to 3
- w_gate: bfloat16 [8192, 16384], P('tensor', 'dp'), may hold values from -0.0625 to 0.0625
- w_up: bfloat16 [8192, 16384], P('tensor', 'dp'), may hold values from -0.0625 to 0.0625
- w_down: bfloat16 [16384, 8192], P('dp', 'tensor'), may hold values from -0.046875 to 0.046875
- mask_gate: int32 [128, 256], P('tensor', 'dp'), may hold values 0 or 1
- mask_up: int32 [128, 256], P('tensor', 'dp'), may hold values 0 or 1
- mask_down: int32 [256, 128], P('dp', 'tensor'), may hold values 0 or 1
Outputs:
- grad_gate: bfloat16 [8192, 16384], P('tensor', 'dp')
- grad_up: bfloat16 [8192, 16384], P('tensor', 'dp')
- grad_down: bfloat16 [16384, 8192], P('dp', 'tensor')
The draws below stay inside these ranges and needn't reach their ends.
All inputs are finite; a program needn't handle non-finite values. No bound on the sum of `mask_gate` or of `mask_up` or of `mask_down` on one device may be relied on, other than what follows from the above.
Results may differ from the reference program's by a relative error of at most 0.014.
Values may be sent and summed in bfloat16 or wider, within the bound.
A program may use at most 256 MiB of HBM per device.

```python
import jax
import jax.numpy as jnp
from jax import lax

D = 8192
F = 16384
BLOCK = 64
TOKENS = 512


def plant(entries, rng, low, largest):
    spot = [jax.random.randint(jax.random.fold_in(rng, axis), (), 0, length) for axis, length in enumerate(entries.shape)]
    widest = entries.shape.index(max(entries.shape))
    next_to = spot[:widest] + [(spot[widest] + 1) % entries.shape[widest]] + spot[widest + 1:]
    return entries.at[tuple(spot)].set(low).at[tuple(next_to)].set(largest)


def steps_of(rng, shape, cuts, smallest, high):
    loudness = 1.0
    for axis_at, parts in cuts:
        steps = jax.random.uniform(jax.random.fold_in(jax.random.fold_in(rng, 6), axis_at), (parts,), jnp.float32, smallest / len(cuts), high / len(cuts))
        loudness = loudness * jnp.repeat(jnp.exp(steps), shape[axis_at] // parts).reshape((-1,) + (1,) * (len(shape) - 1 - axis_at))
    return loudness


def scatter_about(own_key, extent, scale, reach, cuts=(), kind=jnp.bfloat16):
    values = jax.random.normal(own_key, extent, jnp.float32) * scale
    if len(cuts) > 0:
        values = steps_of(own_key, extent, cuts, -0.22, 0.18) * values
    return jnp.clip(values, min=-reach, max=reach).astype(kind)


def setup_inputs(seed: int = 0) -> dict:
    arg_keys = jax.random.split(jax.random.key(seed), 9)
    hidden_in = scatter_about(arg_keys[0], (TOKENS, D), 1.0, 6.0, ((1, 2),))
    teacher = scatter_about(arg_keys[1], (TOKENS, D), 0.5, 3.0, ((1, 2),))
    w_gate = scatter_about(arg_keys[2], (D, F), D ** -0.5, 0.0625, ((0, 2), (1, 16)))
    w_up = scatter_about(arg_keys[3], (D, F), D ** -0.5, 0.0625, ((0, 2), (1, 16)))
    w_down = scatter_about(arg_keys[4], (F, D), F ** -0.5, 0.046875, ((0, 16), (1, 2)))
    mask_gate = plant((jax.random.randint(arg_keys[5], (D // BLOCK, F // BLOCK), 0, 2) < 1).astype(jnp.int32), jax.random.fold_in(arg_keys[5], 1), 0, 1)
    mask_up = plant((jax.random.randint(arg_keys[6], (D // BLOCK, F // BLOCK), 0, 2) < 1).astype(jnp.int32), jax.random.fold_in(arg_keys[6], 1), 0, 1)
    mask_down = plant((jax.random.randint(arg_keys[7], (F // BLOCK, D // BLOCK), 0, 2) < 1).astype(jnp.int32), jax.random.fold_in(arg_keys[7], 1), 0, 1)
    return {"hidden_in": hidden_in, "teacher": teacher, "w_gate": w_gate, "w_up": w_up, "w_down": w_down, "mask_gate": mask_gate, "mask_up": mask_up, "mask_down": mask_down}


def widen(mask):
    return jnp.repeat(jnp.repeat(mask, BLOCK, axis=0), BLOCK, axis=1)


def contract_rows(left, right):
    return lax.dot_general(left, right, (((0,), (0,)), ((), ())), preferred_element_type=jnp.float32)


def reference(hidden_in, teacher, w_gate, w_up, w_down, mask_gate, mask_up, mask_down):
    keep_gate = widen(mask_gate)
    keep_up = widen(mask_up)
    keep_down = widen(mask_down)
    sparse_gate = w_gate * keep_gate.astype(jnp.bfloat16)
    sparse_up = w_up * keep_up.astype(jnp.bfloat16)
    sparse_down = w_down * keep_down.astype(jnp.bfloat16)
    gate = jnp.dot(hidden_in, sparse_gate, preferred_element_type=jnp.float32)
    up = jnp.dot(hidden_in, sparse_up, preferred_element_type=jnp.float32)
    sig = jax.nn.sigmoid(gate)
    act = gate * sig
    hidden = (act * up).astype(jnp.bfloat16)
    student = jnp.dot(hidden, sparse_down, preferred_element_type=jnp.float32)
    residual = (student - teacher.astype(jnp.float32)).astype(jnp.bfloat16)
    grad_down = (contract_rows(hidden, residual) * keep_down.astype(jnp.float32)).astype(jnp.bfloat16)
    grad_hidden = lax.dot_general(residual, sparse_down, (((1,), (1,)), ((), ())), preferred_element_type=jnp.float32)
    grad_act_gate = (grad_hidden * up * sig * (1.0 + gate * (1.0 - sig))).astype(jnp.bfloat16)
    grad_act_up = (grad_hidden * act).astype(jnp.bfloat16)
    grad_gate = (contract_rows(hidden_in, grad_act_gate) * keep_gate.astype(jnp.float32)).astype(jnp.bfloat16)
    grad_up = (contract_rows(hidden_in, grad_act_up) * keep_up.astype(jnp.float32)).astype(jnp.bfloat16)
    return grad_gate, grad_up, grad_down
```

```python
import functools

import jax
import jax.numpy as jnp
from jax import lax
from jax.experimental import pallas as pl
from jax.experimental.pallas import tpu as pltpu
from jax.sharding import PartitionSpec as P

BLOCK = 64
TILE = 512
VMEM = 56 * 1024 * 1024


def widen(mask):
    return jnp.repeat(jnp.repeat(mask, BLOCK, axis=0), BLOCK, axis=1)


def contract_rows(left, right):
    return lax.dot_general(
        left, right, (((0,), (0,)), ((), ())), preferred_element_type=jnp.float32
    )


def contract_cols(left, right):
    return lax.dot_general(
        left, right, (((1,), (1,)), ((), ())), preferred_element_type=jnp.float32
    )


def plain(hidden_in, teacher, w_gate, w_up, w_down, mask_gate, mask_up, mask_down):
    keep_gate = widen(mask_gate)
    keep_up = widen(mask_up)
    keep_down = widen(mask_down)
    sparse_gate = w_gate * keep_gate.astype(jnp.bfloat16)
    sparse_up = w_up * keep_up.astype(jnp.bfloat16)
    sparse_down = w_down * keep_down.astype(jnp.bfloat16)
    gate, up = lax.psum(
        (
            jnp.dot(hidden_in, sparse_gate, preferred_element_type=jnp.float32),
            jnp.dot(hidden_in, sparse_up, preferred_element_type=jnp.float32),
        ),
        "tensor",
    )
    sig = jax.nn.sigmoid(gate)
    act = gate * sig
    hidden_all = (act * up).astype(jnp.bfloat16)
    student = lax.psum(jnp.dot(hidden_all, sparse_down, preferred_element_type=jnp.float32), "dp")
    residual_all = (student - teacher.astype(jnp.float32)).astype(jnp.bfloat16)
    grad_down = (contract_rows(hidden_all, residual_all) * keep_down.astype(jnp.float32)).astype(
        jnp.bfloat16
    )
    grad_hidden = lax.psum(
        contract_cols(residual_all, sparse_down).astype(jnp.bfloat16), "tensor"
    ).astype(jnp.float32)
    grad_act_gate = (grad_hidden * up * sig * (1.0 + gate * (1.0 - sig))).astype(jnp.bfloat16)
    grad_act_up = (grad_hidden * act).astype(jnp.bfloat16)
    gate_total = contract_rows(hidden_in, grad_act_gate)
    up_total = contract_rows(hidden_in, grad_act_up)
    grad_gate = (gate_total * keep_gate.astype(jnp.float32)).astype(jnp.bfloat16)
    grad_up = (up_total * keep_up.astype(jnp.float32)).astype(jnp.bfloat16)
    return (grad_gate, grad_up, grad_down)


def masked(block, mask):
    parts = [
        block[i * BLOCK : (i + 1) * BLOCK] * mask[i : i + 1].astype(block.dtype)
        for i in range(mask.shape[0])
    ]
    return jnp.concatenate(parts, axis=0)


def activations(own_ref, peer_ref):
    gate = own_ref[0] + peer_ref[0].astype(jnp.float32)
    up = own_ref[1] + peer_ref[1].astype(jnp.float32)
    sig = jax.nn.sigmoid(gate)
    return gate, up, sig, gate * sig


def forward_kernel(x_ref, wg_ref, wu_ref, mg_ref, mu_ref, own_ref, send_ref):
    k = pl.program_id(0)
    for i, (w_ref, m_ref) in enumerate(((wg_ref, mg_ref), (wu_ref, mu_ref))):
        part = jnp.dot(
            x_ref[...], masked(w_ref[...], m_ref[...]), preferred_element_type=jnp.float32
        )

        @pl.when(k == 0)
        def _():
            own_ref[i] = part

        @pl.when(k > 0)
        def _():
            own_ref[i] += part

    @pl.when(k == pl.num_programs(0) - 1)
    def _():
        send_ref[...] = own_ref[...].astype(jnp.bfloat16)


def student_kernel(own_ref, peer_ref, wd_ref, md_ref, part_ref, hidden_ref):
    @pl.when(pl.program_id(0) == 0)
    def _():
        _, up, _, act = activations(own_ref, peer_ref)
        hidden_ref[...] = (act * up).astype(jnp.bfloat16)

    part_ref[0] = jnp.dot(
        hidden_ref[...], masked(wd_ref[...], md_ref[...]), preferred_element_type=jnp.float32
    ).astype(jnp.bfloat16)


def residual_kernel(n, part_ref, teacher_ref, out_ref, acc, recv, teach, tsem, ssem, rsem):
    groups, tokens, width = part_ref.shape
    me = lax.axis_index("dp")
    bits = n.bit_length() - 1
    up = list(range(bits))
    swap = [1, 0] + up[2:]
    far = up[2:] + up[:2]
    orders = [(up, swap, far, up, swap, up, swap, far)[g % 8] for g in range(groups)]

    def partner(b):
        return me + (1 - 2 * (lax.rem(me // 2**b, 2))) * 2**b

    barrier = pltpu.get_barrier_semaphore()
    for b in range(bits):
        pl.semaphore_signal(
            barrier, inc=1, device_id={"dp": partner(b)}, device_id_type=pl.DeviceIdType.MESH
        )
    pl.semaphore_wait(barrier, bits)

    def at(start, rows):
        return pl.ds(pl.multiple_of(start, rows), rows)

    copies = []

    def send(g, step, b, src, dst):
        copy = pltpu.make_async_remote_copy(
            src_ref=src,
            dst_ref=dst,
            send_sem=ssem.at[g, step],
            recv_sem=rsem.at[g, step],
            device_id={"dp": partner(b)},
            device_id_type=pl.DeviceIdType.MESH,
        )
        copy.start()
        copies.append(copy)
        return copy

    starts = [[0] for _ in range(groups)]
    for g in range(groups):
        for s in range(bits):
            bit = lax.rem(me // 2 ** orders[g][s], 2)
            starts[g].append(starts[g][s] + bit * (tokens >> (s + 1)))

    def offset(s):
        return tokens - (tokens >> s)

    def halves(g, s):
        half = tokens >> (s + 1)
        bit = lax.rem(me // 2 ** orders[g][s], 2)
        base = 0 if s == 0 else offset(s - 1)
        src = part_ref if s == 0 else acc
        return (
            src.at[g, at(base + bit * half, half)],
            src.at[g, at(base + (1 - bit) * half, half)],
        )

    def scatter(g, s):
        half = tokens >> (s + 1)
        return send(
            g, s, orders[g][s], halves(g, s)[1], recv.at[g, pl.ds(offset(s), half)]
        )

    last = tokens >> bits
    pending = [scatter(g, 0) for g in range(groups)]
    teachers = []
    for g in range(groups):
        copy = pltpu.make_async_copy(
            teacher_ref.at[at(starts[g][bits], last), pl.ds(g * width, width)],
            teach.at[g],
            tsem.at[g],
        )
        copy.start()
        teachers.append(copy)

    for s in range(bits):
        half = tokens >> (s + 1)
        for g in range(groups):
            pending[g].wait_recv()
            kept = halves(g, s)[0][...].astype(jnp.float32)
            total = kept + recv[g, pl.ds(offset(s), half)].astype(jnp.float32)
            if s < bits - 1:
                acc[g, pl.ds(offset(s), half)] = total.astype(jnp.bfloat16)
                pending[g] = scatter(g, s + 1)
            else:
                teachers[g].wait()
                rows = at(starts[g][bits], last)
                out_ref[g, rows] = (total - teach[g].astype(jnp.float32)).astype(jnp.bfloat16)
                here = out_ref.at[g, rows]
                pending[g] = send(g, bits, orders[g][s], here, here)
    for t in range(1, bits + 1):
        for g in range(groups):
            pending[g].wait_recv()
            if t < bits:
                s = bits - 1 - t
                here = out_ref.at[g, at(starts[g][s + 1], tokens >> (s + 1))]
                pending[g] = send(g, bits + t, orders[g][s], here, here)
    for copy in copies:
        copy.wait_send()


def down_kernel(res_ref, hidden_ref, wd_ref, md_ref, gd_ref, gh_ref, send_ref, turned):
    k = pl.program_id(0)

    @pl.when(k == 0)
    def _():
        turned[...] = hidden_ref[...].T

    res = res_ref[0]
    mask = md_ref[...]
    gd = jnp.dot(turned[...], res, preferred_element_type=jnp.float32)
    gd_ref[...] = masked(gd, mask).astype(jnp.bfloat16)
    gh = contract_cols(res, masked(wd_ref[...], mask))

    @pl.when(k == 0)
    def _():
        gh_ref[...] = gh

    @pl.when(k > 0)
    def _():
        gh_ref[...] += gh

    @pl.when(k == pl.num_programs(0) - 1)
    def _():
        send_ref[...] = gh_ref[...].astype(jnp.bfloat16)


def weights_kernel(
    own_ref, peer_ref, gh_ref, gh_peer_ref, x_ref, mg_ref, mu_ref, gg_ref, gu_ref, grads
):
    hidden = gg_ref.shape[1]

    @pl.when(pl.program_id(0) == 0)
    def _():
        gate, up, sig, act = activations(own_ref, peer_ref)
        gh = gh_ref[...] + gh_peer_ref[...].astype(jnp.float32)
        grads[:, :hidden] = (gh * up * sig * (1.0 + gate * (1.0 - sig))).astype(jnp.bfloat16)
        grads[:, hidden:] = (gh * act).astype(jnp.bfloat16)

    turned = x_ref[...].T
    for i, (m_ref, out_ref) in enumerate(((mg_ref, gg_ref), (mu_ref, gu_ref))):
        total = jnp.dot(
            turned, grads[:, i * hidden : (i + 1) * hidden], preferred_element_type=jnp.float32
        )
        out_ref[...] = masked(total, m_ref[...]).astype(jnp.bfloat16)


def params(**more):
    return pltpu.CompilerParams(vmem_limit_bytes=VMEM, **more)


def whole(shape):
    return pl.BlockSpec(shape, lambda k: (0,) * len(shape))


def with_kernels(n, hidden_in, teacher, w_gate, w_up, w_down, mask_gate, mask_up, mask_down):
    tokens, depth = hidden_in.shape
    units = w_gate.shape[1]
    tile = TILE
    steps = depth // tile
    f32, bf16 = jnp.float32, jnp.bfloat16
    rows = tile // BLOCK
    shape = jax.ShapeDtypeStruct
    wide_gate = jnp.repeat(mask_gate.astype(f32), BLOCK, axis=1)
    wide_up = jnp.repeat(mask_up.astype(f32), BLOCK, axis=1)
    wide_down = jnp.repeat(mask_down.astype(f32), BLOCK, axis=1)
    x_spec = pl.BlockSpec((tokens, tile), lambda k: (0, k))
    w_spec = pl.BlockSpec((tile, units), lambda k: (k, 0))
    m_spec = pl.BlockSpec((rows, units), lambda k: (k, 0))
    wd_spec = pl.BlockSpec((units, tile), lambda k: (0, k))
    md_spec = pl.BlockSpec((units // BLOCK, tile), lambda k: (0, k))
    part_spec = pl.BlockSpec((1, tokens, tile), lambda k: (k, 0, 0))
    both, one = (2, tokens, units), (tokens, units)
    product = 2 * tokens * depth * units

    def cost(products, moved):
        return pl.CostEstimate(flops=products * product, bytes_accessed=moved, transcendentals=0)

    own, mine = pl.pallas_call(
        forward_kernel,
        grid=(steps,),
        in_specs=[x_spec, w_spec, w_spec, m_spec, m_spec],
        out_specs=[whole(both), whole(both)],
        out_shape=[shape(both, f32), shape(both, bf16)],
        compiler_params=params(),
        cost_estimate=cost(2, 4 * depth * units),
    )(hidden_in, w_gate, w_up, wide_gate, wide_up)
    peer = lax.ppermute(mine, "tensor", [(0, 1), (1, 0)])
    partial, hidden = pl.pallas_call(
        student_kernel,
        grid=(steps,),
        in_specs=[whole(both), whole(both), wd_spec, md_spec],
        out_specs=[part_spec, whole(one)],
        out_shape=[shape((steps, tokens, tile), bf16), shape(one, bf16)],
        compiler_params=params(),
        cost_estimate=cost(1, 2 * depth * units),
    )(own, peer, w_down, wide_down)
    bits = n.bit_length() - 1
    residual = pl.pallas_call(
        functools.partial(residual_kernel, n),
        in_specs=[pl.BlockSpec(memory_space=pltpu.VMEM), pl.BlockSpec(memory_space=pl.ANY)],
        out_specs=pl.BlockSpec(memory_space=pltpu.VMEM),
        out_shape=shape((steps, tokens, tile), bf16),
        scratch_shapes=[
            pltpu.VMEM((steps, tokens, tile), bf16),
            pltpu.VMEM((steps, tokens, tile), bf16),
            pltpu.VMEM((steps, tokens // n, tile), bf16),
            pltpu.SemaphoreType.DMA((steps,)),
            pltpu.SemaphoreType.DMA((steps, 2 * bits)),
            pltpu.SemaphoreType.DMA((steps, 2 * bits)),
        ],
        compiler_params=params(collective_id=0, has_side_effects=True),
    )(partial, teacher)
    grad_down, gh, gh_mine = pl.pallas_call(
        down_kernel,
        grid=(steps,),
        in_specs=[part_spec, whole(one), wd_spec, md_spec],
        out_specs=[wd_spec, whole(one), whole(one)],
        out_shape=[shape((units, depth), bf16), shape(one, f32), shape(one, bf16)],
        scratch_shapes=[pltpu.VMEM((units, tokens), bf16)],
        compiler_params=params(),
        cost_estimate=cost(2, 4 * depth * units),
    )(residual, hidden, w_down, wide_down)
    gh_peer = lax.ppermute(gh_mine, "tensor", [(0, 1), (1, 0)])
    grad_gate, grad_up = pl.pallas_call(
        weights_kernel,
        grid=(steps,),
        in_specs=[whole(both), whole(both), whole(one), whole(one), x_spec, m_spec, m_spec],
        out_specs=[w_spec, w_spec],
        out_shape=[shape((depth, units), bf16)] * 2,
        scratch_shapes=[pltpu.VMEM((tokens, 2 * units), bf16)],
        compiler_params=params(),
        cost_estimate=cost(2, 4 * depth * units),
    )(own, peer, gh, gh_peer, hidden_in, wide_gate, wide_up)
    return (grad_gate, grad_up, grad_down)


def on_device(n, tensor, *args):
    tokens, depth = args[0].shape
    units = args[2].shape[1]
    fits = tensor == 2 and n >= 4 and n & (n - 1) == 0 and tokens % (16 * n) == 0
    if fits and depth % TILE == 0 and units % 256 == 0:
        return with_kernels(n, *args)
    return plain(*args)


def solution(mesh):
    in_specs = (
        P(None, "tensor"),
        P(None, "tensor"),
        P("tensor", "dp"),
        P("tensor", "dp"),
        P("dp", "tensor"),
        P("tensor", "dp"),
        P("tensor", "dp"),
        P("dp", "tensor"),
    )
    out_specs = (P("tensor", "dp"), P("tensor", "dp"), P("dp", "tensor"))
    return jax.shard_map(
        functools.partial(on_device, mesh.shape["dp"], mesh.shape["tensor"]),
        mesh=mesh,
         in_specs=in_specs, out_specs=out_specs, check_vma=False
    )
```

```python
import functools

import jax
import jax.numpy as jnp
from jax import lax
from jax.experimental import pallas as pl
from jax.experimental.pallas import tpu as pltpu
from jax.sharding import PartitionSpec as P

BLOCK = 64
TILE = 512
VMEM = 56 * 1024 * 1024


def widen(mask):
    return jnp.repeat(jnp.repeat(mask, BLOCK, axis=0), BLOCK, axis=1)


def contract_rows(left, right):
    return lax.dot_general(
        left, right, (((0,), (0,)), ((), ())), preferred_element_type=jnp.float32
    )


def contract_cols(left, right):
    return lax.dot_general(
        left, right, (((1,), (1,)), ((), ())), preferred_element_type=jnp.float32
    )


def plain(hidden_in, teacher, w_gate, w_up, w_down, mask_gate, mask_up, mask_down):
    keep_gate = widen(mask_gate)
    keep_up = widen(mask_up)
    keep_down = widen(mask_down)
    sparse_gate = w_gate * keep_gate.astype(jnp.bfloat16)
    sparse_up = w_up * keep_up.astype(jnp.bfloat16)
    sparse_down = w_down * keep_down.astype(jnp.bfloat16)
    gate, up = lax.psum(
        (
            jnp.dot(hidden_in, sparse_gate, preferred_element_type=jnp.float32),
            jnp.dot(hidden_in, sparse_up, preferred_element_type=jnp.float32),
        ),
        "tensor",
    )
    sig = jax.nn.sigmoid(gate)
    act = gate * sig
    hidden_all = (act * up).astype(jnp.bfloat16)
    student = lax.psum(jnp.dot(hidden_all, sparse_down, preferred_element_type=jnp.float32), "dp")
    residual_all = (student - teacher.astype(jnp.float32)).astype(jnp.bfloat16)
    grad_down = (contract_rows(hidden_all, residual_all) * keep_down.astype(jnp.float32)).astype(
        jnp.bfloat16
    )
    grad_hidden = lax.psum(
        contract_cols(residual_all, sparse_down).astype(jnp.bfloat16), "tensor"
    ).astype(jnp.float32)
    grad_act_gate = (grad_hidden * up * sig * (1.0 + gate * (1.0 - sig))).astype(jnp.bfloat16)
    grad_act_up = (grad_hidden * act).astype(jnp.bfloat16)
    gate_total = contract_rows(hidden_in, grad_act_gate)
    up_total = contract_rows(hidden_in, grad_act_up)
    grad_gate = (gate_total * keep_gate.astype(jnp.float32)).astype(jnp.bfloat16)
    grad_up = (up_total * keep_up.astype(jnp.float32)).astype(jnp.bfloat16)
    return (grad_gate, grad_up, grad_down)


def masked(block, mask):
    parts = [
        block[i * BLOCK : (i + 1) * BLOCK] * mask[i : i + 1].astype(block.dtype)
        for i in range(mask.shape[0])
    ]
    return jnp.concatenate(parts, axis=0)


def widened(mask, first, width):
    shape = (mask.shape[1], width)
    column = lax.div(lax.broadcasted_iota(jnp.int32, shape, 1), BLOCK) + first
    pick = (lax.broadcasted_iota(jnp.int32, shape, 0) == column).astype(jnp.bfloat16)
    return jnp.dot(
        mask.astype(jnp.float32).astype(jnp.bfloat16), pick, preferred_element_type=jnp.float32
    )


def activations(own_ref, peer_ref):
    gate = own_ref[0] + peer_ref[0].astype(jnp.float32)
    up = own_ref[1] + peer_ref[1].astype(jnp.float32)
    sig = jax.nn.sigmoid(gate)
    return gate, up, sig, gate * sig


def forward_kernel(x_ref, wg_ref, wu_ref, mg_ref, mu_ref, own_ref, send_ref):
    k = pl.program_id(0)
    for i, (w_ref, m_ref) in enumerate(((wg_ref, mg_ref), (wu_ref, mu_ref))):
        mask = widened(m_ref[...], 0, w_ref.shape[1])
        part = jnp.dot(
            x_ref[...], masked(w_ref[...], mask), preferred_element_type=jnp.float32
        )

        @pl.when(k == 0)
        def _():
            own_ref[i] = part

        @pl.when(k > 0)
        def _():
            own_ref[i] += part

    @pl.when(k == pl.num_programs(0) - 1)
    def _():
        send_ref[...] = own_ref[...].astype(jnp.bfloat16)


def residual_kernel(
    n,
    own_ref,
    peer_ref,
    md_ref,
    wd_ref,
    teacher_ref,
    out_ref,
    turned_ref,
    factors_ref,
    gh_ref,
    gh_send_ref,
    hidden,
    part_ref,
    sparse,
    acc,
    recv,
    teach,
    wsem,
    tsem,
    ssem,
    rsem,
):
    groups, tokens, width = part_ref.shape
    weights = []
    for g in range(groups):
        copy = pltpu.make_async_copy(
            wd_ref.at[:, pl.ds(g * width, width)], sparse.at[g], wsem.at[g]
        )
        copy.start()
        weights.append(copy)
    me = lax.axis_index("dp")
    bits = n.bit_length() - 1
    near = list(range(bits))
    swap = [1, 0] + near[2:]
    far = near[2:] + near[:2]
    orders = [(near, swap, far, near, swap, near, swap, far)[g % 8] for g in range(groups)]

    def partner(b):
        return me + (1 - 2 * (lax.rem(me // 2**b, 2))) * 2**b

    barrier = pltpu.get_barrier_semaphore()
    for b in range(bits):
        pl.semaphore_signal(
            barrier, inc=1, device_id={"dp": partner(b)}, device_id_type=pl.DeviceIdType.MESH
        )
    _, up_sum, _, act = activations(own_ref, peer_ref)
    hidden[...] = (act * up_sum).astype(jnp.bfloat16)
    pl.semaphore_wait(barrier, bits)

    def at(start, rows):
        return pl.ds(pl.multiple_of(start, rows), rows)

    copies = []

    def send(g, step, b, src, dst):
        copy = pltpu.make_async_remote_copy(
            src_ref=src,
            dst_ref=dst,
            send_sem=ssem.at[g, step],
            recv_sem=rsem.at[g, step],
            device_id={"dp": partner(b)},
            device_id_type=pl.DeviceIdType.MESH,
        )
        copy.start()
        copies.append(copy)
        return copy

    starts = [[0] for _ in range(groups)]
    for g in range(groups):
        for s in range(bits):
            bit = lax.rem(me // 2 ** orders[g][s], 2)
            starts[g].append(starts[g][s] + bit * (tokens >> (s + 1)))

    def offset(s):
        return tokens - (tokens >> s)

    def halves(g, s):
        half = tokens >> (s + 1)
        bit = lax.rem(me // 2 ** orders[g][s], 2)
        base = 0 if s == 0 else offset(s - 1)
        src = part_ref if s == 0 else acc
        return (
            src.at[g, at(base + bit * half, half)],
            src.at[g, at(base + (1 - bit) * half, half)],
        )

    def scatter(g, s):
        half = tokens >> (s + 1)
        return send(
            g, s, orders[g][s], halves(g, s)[1], recv.at[g, pl.ds(offset(s), half)]
        )

    last = tokens >> bits
    pending = []
    for g in range(groups):
        weights[g].wait()
        mask = widened(md_ref[...], g * (width // BLOCK), width)
        sparse[g] = masked(sparse[g], mask)
        part_ref[g] = jnp.dot(
            hidden[...], sparse[g], preferred_element_type=jnp.float32
        ).astype(jnp.bfloat16)
        pending.append(scatter(g, 0))
    teachers = []
    for g in range(groups):
        copy = pltpu.make_async_copy(
            teacher_ref.at[at(starts[g][bits], last), pl.ds(g * width, width)],
            teach.at[g],
            tsem.at[g],
        )
        copy.start()
        teachers.append(copy)
    turned_ref[...] = hidden[...].T
    gate, up_sum, sig, act = activations(own_ref, peer_ref)
    factors_ref[0] = up_sum * sig * (1.0 + gate * (1.0 - sig))
    factors_ref[1] = act

    for s in range(bits):
        half = tokens >> (s + 1)
        for g in range(groups):
            pending[g].wait_recv()
            kept = halves(g, s)[0][...].astype(jnp.float32)
            total = kept + recv[g, pl.ds(offset(s), half)].astype(jnp.float32)
            if s < bits - 1:
                acc[g, pl.ds(offset(s), half)] = total.astype(jnp.bfloat16)
                pending[g] = scatter(g, s + 1)
            else:
                teachers[g].wait()
                rows = at(starts[g][bits], last)
                out_ref[g, rows] = (total - teach[g].astype(jnp.float32)).astype(jnp.bfloat16)
                here = out_ref.at[g, rows]
                pending[g] = send(g, bits, orders[g][s], here, here)
    for t in range(1, bits + 1):
        for g in range(groups):
            pending[g].wait_recv()
            if t < bits:
                s = bits - 1 - t
                here = out_ref.at[g, at(starts[g][s + 1], tokens >> (s + 1))]
                pending[g] = send(g, bits + t, orders[g][s], here, here)
            else:
                share = contract_cols(out_ref[g], sparse[g])
                if g == 0:
                    gh_ref[...] = share
                else:
                    gh_ref[...] += share
    gh_send_ref[...] = gh_ref[...].astype(jnp.bfloat16)
    for copy in copies:
        copy.wait_send()


def down_kernel(turned_ref, res_ref, md_ref, gd_ref):
    width = gd_ref.shape[1]
    mask = widened(md_ref[...], pl.program_id(0) * (width // BLOCK), width)
    total = jnp.dot(turned_ref[...], res_ref[0], preferred_element_type=jnp.float32)
    gd_ref[...] = masked(total.astype(jnp.bfloat16), mask)


def weights_kernel(
    factors_ref, gh_ref, gh_peer_ref, x_ref, mg_ref, mu_ref, gg_ref, gu_ref, grads
):
    hidden = gg_ref.shape[1]

    @pl.when(pl.program_id(0) == 0)
    def _():
        gh = gh_ref[...] + gh_peer_ref[...].astype(jnp.float32)
        grads[:, :hidden] = (gh * factors_ref[0]).astype(jnp.bfloat16)
        grads[:, hidden:] = (gh * factors_ref[1]).astype(jnp.bfloat16)

    turned = x_ref[...].T
    for i, (m_ref, out_ref) in enumerate(((mg_ref, gg_ref), (mu_ref, gu_ref))):
        total = jnp.dot(
            turned, grads[:, i * hidden : (i + 1) * hidden], preferred_element_type=jnp.float32
        )
        out_ref[...] = masked(total.astype(jnp.bfloat16), widened(m_ref[...], 0, hidden))


def params(**more):
    return pltpu.CompilerParams(vmem_limit_bytes=VMEM, **more)


def whole(shape):
    return pl.BlockSpec(shape, lambda k: (0,) * len(shape))


def with_kernels(n, hidden_in, teacher, w_gate, w_up, w_down, mask_gate, mask_up, mask_down):
    tokens, depth = hidden_in.shape
    units = w_gate.shape[1]
    tile = TILE
    steps = depth // tile
    f32, bf16 = jnp.float32, jnp.bfloat16
    shape = jax.ShapeDtypeStruct
    both, one = (2, tokens, units), (tokens, units)
    product = 2 * tokens * depth * units

    def cost(products, moved):
        return pl.CostEstimate(flops=products * product, bytes_accessed=moved, transcendentals=0)

    def specs(tile):
        return (
            pl.BlockSpec((tokens, tile), lambda k: (0, k)),
            pl.BlockSpec((tile, units), lambda k: (k, 0)),
            pl.BlockSpec((tile // BLOCK, units // BLOCK), lambda k: (k, 0)),
        )

    x_spec, w_spec, m_spec = specs(2 * tile)
    own, mine = pl.pallas_call(
        forward_kernel,
        grid=(steps // 2,),
        in_specs=[x_spec, w_spec, w_spec, m_spec, m_spec],
        out_specs=[whole(both), whole(both)],
        out_shape=[shape(both, f32), shape(both, bf16)],
        compiler_params=params(),
        cost_estimate=cost(2, 4 * depth * units),
    )(hidden_in, w_gate, w_up, mask_gate, mask_up)
    peer = lax.ppermute(mine, "tensor", [(0, 1), (1, 0)])
    bits = n.bit_length() - 1
    vmem = pl.BlockSpec(memory_space=pltpu.VMEM)
    hbm = pl.BlockSpec(memory_space=pl.ANY)
    groups = (steps, tokens, tile)
    residual, turned, factors, gh, gh_mine = pl.pallas_call(
        functools.partial(residual_kernel, n),
        in_specs=[vmem, vmem, vmem, hbm, hbm],
        out_specs=[vmem] * 5,
        out_shape=[
            shape(groups, bf16),
            shape((units, tokens), bf16),
            shape(both, f32),
            shape(one, f32),
            shape(one, bf16),
        ],
        scratch_shapes=[
            pltpu.VMEM(one, bf16),
            pltpu.VMEM(groups, bf16),
            pltpu.VMEM((steps, units, tile), bf16),
            pltpu.VMEM(groups, bf16),
            pltpu.VMEM(groups, bf16),
            pltpu.VMEM((steps, tokens // n, tile), bf16),
            pltpu.SemaphoreType.DMA((steps,)),
            pltpu.SemaphoreType.DMA((steps,)),
            pltpu.SemaphoreType.DMA((steps, 2 * bits)),
            pltpu.SemaphoreType.DMA((steps, 2 * bits)),
        ],
        compiler_params=params(collective_id=0, has_side_effects=True),
    )(own, peer, mask_down, w_down, teacher)
    gh_peer = lax.ppermute(gh_mine, "tensor", [(0, 1), (1, 0)])
    grad_down = pl.pallas_call(
        down_kernel,
        grid=(steps,),
        in_specs=[
            whole((units, tokens)),
            pl.BlockSpec((1, tokens, tile), lambda k: (k, 0, 0)),
            whole(mask_down.shape),
        ],
        out_specs=pl.BlockSpec((units, tile), lambda k: (0, k)),
        out_shape=shape((units, depth), bf16),
        compiler_params=params(),
        cost_estimate=cost(1, 2 * depth * units),
    )(turned, residual, mask_down)
    x_spec, w_spec, m_spec = specs(tile)
    grad_gate, grad_up = pl.pallas_call(
        weights_kernel,
        grid=(steps,),
        in_specs=[whole(both), whole(one), whole(one), x_spec, m_spec, m_spec],
        out_specs=[w_spec, w_spec],
        out_shape=[shape((depth, units), bf16)] * 2,
        scratch_shapes=[pltpu.VMEM((tokens, 2 * units), bf16)],
        compiler_params=params(),
        cost_estimate=cost(2, 4 * depth * units),
    )(factors, gh, gh_peer, hidden_in, mask_gate, mask_up)
    return (grad_gate, grad_up, grad_down)


def on_device(n, tensor, *args):
    tokens, depth = args[0].shape
    units = args[2].shape[1]
    fits = tensor == 2 and n >= 4 and n & (n - 1) == 0 and tokens % (16 * n) == 0
    if fits and depth % (2 * TILE) == 0 and units % 256 == 0:
        return with_kernels(n, *args)
    return plain(*args)


def solution(mesh):
    in_specs = (
        P(None, "tensor"),
        P(None, "tensor"),
        P("tensor", "dp"),
        P("tensor", "dp"),
        P("dp", "tensor"),
        P("tensor", "dp"),
        P("tensor", "dp"),
        P("dp", "tensor"),
    )
    out_specs = (P("tensor", "dp"), P("tensor", "dp"), P("dp", "tensor"))
    return jax.shard_map(
        functools.partial(on_device, mesh.shape["dp"], mesh.shape["tensor"]),
        mesh=mesh,
         in_specs=in_specs, out_specs=out_specs, check_vma=False
    )
```

```python
import functools

import jax
import jax.numpy as jnp
from jax import lax
from jax.experimental import pallas as pl
from jax.experimental.pallas import tpu as pltpu
from jax.sharding import PartitionSpec as P

BLOCK = 64
TILE = 512
VMEM = 56 * 1024 * 1024


def widen(mask):
    return jnp.repeat(jnp.repeat(mask, BLOCK, axis=0), BLOCK, axis=1)


def contract_rows(left, right):
    return lax.dot_general(
        left, right, (((0,), (0,)), ((), ())), preferred_element_type=jnp.float32
    )


def contract_cols(left, right):
    return lax.dot_general(
        left, right, (((1,), (1,)), ((), ())), preferred_element_type=jnp.float32
    )


def plain(hidden_in, teacher, w_gate, w_up, w_down, mask_gate, mask_up, mask_down):
    keep_gate = widen(mask_gate)
    keep_up = widen(mask_up)
    keep_down = widen(mask_down)
    sparse_gate = w_gate * keep_gate.astype(jnp.bfloat16)
    sparse_up = w_up * keep_up.astype(jnp.bfloat16)
    sparse_down = w_down * keep_down.astype(jnp.bfloat16)
    gate, up = lax.psum(
        (
            jnp.dot(hidden_in, sparse_gate, preferred_element_type=jnp.float32),
            jnp.dot(hidden_in, sparse_up, preferred_element_type=jnp.float32),
        ),
        "tensor",
    )
    sig = jax.nn.sigmoid(gate)
    act = gate * sig
    hidden_all = (act * up).astype(jnp.bfloat16)
    student = lax.psum(jnp.dot(hidden_all, sparse_down, preferred_element_type=jnp.float32), "dp")
    residual_all = (student - teacher.astype(jnp.float32)).astype(jnp.bfloat16)
    grad_down = (contract_rows(hidden_all, residual_all) * keep_down.astype(jnp.float32)).astype(
        jnp.bfloat16
    )
    grad_hidden = lax.psum(
        contract_cols(residual_all, sparse_down).astype(jnp.bfloat16), "tensor"
    ).astype(jnp.float32)
    grad_act_gate = (grad_hidden * up * sig * (1.0 + gate * (1.0 - sig))).astype(jnp.bfloat16)
    grad_act_up = (grad_hidden * act).astype(jnp.bfloat16)
    gate_total = contract_rows(hidden_in, grad_act_gate)
    up_total = contract_rows(hidden_in, grad_act_up)
    grad_gate = (gate_total * keep_gate.astype(jnp.float32)).astype(jnp.bfloat16)
    grad_up = (up_total * keep_up.astype(jnp.float32)).astype(jnp.bfloat16)
    return (grad_gate, grad_up, grad_down)


def masked(block, mask):
    parts = [
        block[i * BLOCK : (i + 1) * BLOCK] * mask[i : i + 1].astype(block.dtype)
        for i in range(mask.shape[0])
    ]
    return jnp.concatenate(parts, axis=0)


def widened(mask, first, width):
    shape = (mask.shape[1], width)
    column = lax.div(lax.broadcasted_iota(jnp.int32, shape, 1), BLOCK) + first
    pick = (lax.broadcasted_iota(jnp.int32, shape, 0) == column).astype(jnp.bfloat16)
    return jnp.dot(
        mask.astype(jnp.float32).astype(jnp.bfloat16), pick, preferred_element_type=jnp.float32
    )


def activations(own_ref, peer_ref):
    gate = own_ref[0] + peer_ref[0].astype(jnp.float32)
    up = own_ref[1] + peer_ref[1].astype(jnp.float32)
    sig = jax.nn.sigmoid(gate)
    return gate, up, sig, gate * sig


def forward_kernel(x_ref, wg_ref, wu_ref, mg_ref, mu_ref, own_ref, send_ref):
    k = pl.program_id(0)
    for i, (w_ref, m_ref) in enumerate(((wg_ref, mg_ref), (wu_ref, mu_ref))):
        mask = widened(m_ref[...], 0, w_ref.shape[1])
        part = jnp.dot(
            x_ref[...], masked(w_ref[...], mask), preferred_element_type=jnp.float32
        )

        @pl.when(k == 0)
        def _():
            own_ref[i] = part

        @pl.when(k > 0)
        def _():
            own_ref[i] += part

    @pl.when(k == pl.num_programs(0) - 1)
    def _():
        send_ref[...] = own_ref[...].astype(jnp.bfloat16)


def residual_kernel(
    n,
    own_ref,
    peer_ref,
    md_ref,
    wd_ref,
    teacher_ref,
    out_ref,
    turned_ref,
    factors_ref,
    gh_ref,
    gh_send_ref,
    hidden,
    part_ref,
    sparse,
    acc,
    recv,
    teach,
    wsem,
    tsem,
    ssem,
    rsem,
):
    groups, tokens, width = part_ref.shape
    weights = []
    for g in range(groups):
        copy = pltpu.make_async_copy(
            wd_ref.at[:, pl.ds(g * width, width)], sparse.at[g], wsem.at[g]
        )
        copy.start()
        weights.append(copy)
    me = lax.axis_index("dp")
    bits = n.bit_length() - 1
    near = list(range(bits))
    swap = [1, 0] + near[2:]
    far = near[2:] + near[:2]
    orders = [(near, swap, far, near, swap, near, swap, far)[g % 8] for g in range(groups)]

    def partner(b):
        return me + (1 - 2 * (lax.rem(me // 2**b, 2))) * 2**b

    barrier = pltpu.get_barrier_semaphore()
    for b in range(bits):
        pl.semaphore_signal(
            barrier, inc=1, device_id={"dp": partner(b)}, device_id_type=pl.DeviceIdType.MESH
        )
    _, up_sum, _, act = activations(own_ref, peer_ref)
    hidden[...] = (act * up_sum).astype(jnp.bfloat16)
    pl.semaphore_wait(barrier, bits)

    def at(start, rows):
        return pl.ds(pl.multiple_of(start, rows), rows)

    copies = []

    def send(g, step, b, src, dst):
        copy = pltpu.make_async_remote_copy(
            src_ref=src,
            dst_ref=dst,
            send_sem=ssem.at[g, step],
            recv_sem=rsem.at[g, step],
            device_id={"dp": partner(b)},
            device_id_type=pl.DeviceIdType.MESH,
        )
        copy.start()
        copies.append(copy)
        return copy

    starts = [[0] for _ in range(groups)]
    for g in range(groups):
        for s in range(bits):
            bit = lax.rem(me // 2 ** orders[g][s], 2)
            starts[g].append(starts[g][s] + bit * (tokens >> (s + 1)))

    def offset(s):
        return tokens - (tokens >> s)

    def halves(g, s):
        half = tokens >> (s + 1)
        bit = lax.rem(me // 2 ** orders[g][s], 2)
        base = 0 if s == 0 else offset(s - 1)
        src = part_ref if s == 0 else acc
        return (
            src.at[g, at(base + bit * half, half)],
            src.at[g, at(base + (1 - bit) * half, half)],
        )

    def scatter(g, s):
        half = tokens >> (s + 1)
        return send(
            g, s, orders[g][s], halves(g, s)[1], recv.at[g, pl.ds(offset(s), half)]
        )

    last = tokens >> bits
    pending = []
    for g in range(groups):
        weights[g].wait()
        mask = widened(md_ref[...], g * (width // BLOCK), width)
        sparse[g] = masked(sparse[g], mask)
        part_ref[g] = jnp.dot(
            hidden[...], sparse[g], preferred_element_type=jnp.float32
        ).astype(jnp.bfloat16)
        pending.append(scatter(g, 0))
    teachers = []
    for g in range(groups):
        copy = pltpu.make_async_copy(
            teacher_ref.at[at(starts[g][bits], last), pl.ds(g * width, width)],
            teach.at[g],
            tsem.at[g],
        )
        copy.start()
        teachers.append(copy)
    turned_ref[...] = hidden[...].T
    gate, up_sum, sig, act = activations(own_ref, peer_ref)
    factors_ref[0] = up_sum * sig * (1.0 + gate * (1.0 - sig))
    factors_ref[1] = act

    for s in range(bits):
        half = tokens >> (s + 1)
        for g in range(groups):
            pending[g].wait_recv()
            kept = halves(g, s)[0][...].astype(jnp.float32)
            total = kept + recv[g, pl.ds(offset(s), half)].astype(jnp.float32)
            if s < bits - 1:
                acc[g, pl.ds(offset(s), half)] = total.astype(jnp.bfloat16)
                pending[g] = scatter(g, s + 1)
            else:
                teachers[g].wait()
                rows = at(starts[g][bits], last)
                out_ref[g, rows] = (total - teach[g].astype(jnp.float32)).astype(jnp.bfloat16)
                here = out_ref.at[g, rows]
                pending[g] = send(g, bits, orders[g][s], here, here)
    for t in range(1, bits + 1):
        for g in range(groups):
            pending[g].wait_recv()
            if t < bits:
                s = bits - 1 - t
                here = out_ref.at[g, at(starts[g][s + 1], tokens >> (s + 1))]
                pending[g] = send(g, bits + t, orders[g][s], here, here)
            else:
                share = contract_cols(out_ref[g], sparse[g])
                if g == 0:
                    gh_ref[...] = share
                else:
                    gh_ref[...] += share
    gh_send_ref[...] = gh_ref[...].astype(jnp.bfloat16)
    for copy in copies:
        copy.wait_send()


def down_kernel(turned_ref, res_ref, md_ref, gd_ref):
    width = gd_ref.shape[1]
    mask = widened(md_ref[...], pl.program_id(0) * (width // BLOCK), width)
    total = jnp.dot(turned_ref[...], res_ref[0], preferred_element_type=jnp.float32)
    gd_ref[...] = masked(total.astype(jnp.bfloat16), mask)


def weights_kernel(
    factors_ref, gh_ref, gh_peer_ref, x_ref, mg_ref, mu_ref, gg_ref, gu_ref, grads, keep
):
    hidden = gg_ref.shape[1]

    @pl.when(pl.program_id(0) == 0)
    def _():
        gh = gh_ref[...] + gh_peer_ref[...].astype(jnp.float32)
        grads[:, :hidden] = (gh * factors_ref[0]).astype(jnp.bfloat16)
        keep[0] = widened(mg_ref[...], 0, hidden)
        keep[1] = widened(mu_ref[...], 0, hidden)
        grads[:, hidden:] = (gh * factors_ref[1]).astype(jnp.bfloat16)

    turned = x_ref[...].T
    rows = gg_ref.shape[0] // BLOCK
    first = pl.multiple_of(pl.program_id(0) * rows, rows)
    for i, out_ref in enumerate((gg_ref, gu_ref)):
        total = jnp.dot(
            turned, grads[:, i * hidden : (i + 1) * hidden], preferred_element_type=jnp.float32
        )
        out_ref[...] = masked(total, keep[i, pl.ds(first, rows)]).astype(jnp.bfloat16)


def params(**more):
    return pltpu.CompilerParams(vmem_limit_bytes=VMEM, **more)


def whole(shape):
    return pl.BlockSpec(shape, lambda k: (0,) * len(shape))


def with_kernels(n, hidden_in, teacher, w_gate, w_up, w_down, mask_gate, mask_up, mask_down):
    tokens, depth = hidden_in.shape
    units = w_gate.shape[1]
    tile = TILE
    steps = depth // tile
    f32, bf16 = jnp.float32, jnp.bfloat16
    shape = jax.ShapeDtypeStruct
    both, one = (2, tokens, units), (tokens, units)
    product = 2 * tokens * depth * units

    def cost(products, moved):
        return pl.CostEstimate(flops=products * product, bytes_accessed=moved, transcendentals=0)

    def specs(tile):
        return (
            pl.BlockSpec((tokens, tile), lambda k: (0, k)),
            pl.BlockSpec((tile, units), lambda k: (k, 0)),
            pl.BlockSpec((tile // BLOCK, units // BLOCK), lambda k: (k, 0)),
        )

    x_spec, w_spec, m_spec = specs(2 * tile)
    own, mine = pl.pallas_call(
        forward_kernel,
        grid=(steps // 2,),
        in_specs=[x_spec, w_spec, w_spec, m_spec, m_spec],
        out_specs=[whole(both), whole(both)],
        out_shape=[shape(both, f32), shape(both, bf16)],
        compiler_params=params(),
        cost_estimate=cost(2, 4 * depth * units),
    )(hidden_in, w_gate, w_up, mask_gate, mask_up)
    peer = lax.ppermute(mine, "tensor", [(0, 1), (1, 0)])
    bits = n.bit_length() - 1
    vmem = pl.BlockSpec(memory_space=pltpu.VMEM)
    hbm = pl.BlockSpec(memory_space=pl.ANY)
    groups = (steps, tokens, tile)
    residual, turned, factors, gh, gh_mine = pl.pallas_call(
        functools.partial(residual_kernel, n),
        in_specs=[vmem, vmem, vmem, hbm, hbm],
        out_specs=[vmem] * 5,
        out_shape=[
            shape(groups, bf16),
            shape((units, tokens), bf16),
            shape(both, f32),
            shape(one, f32),
            shape(one, bf16),
        ],
        scratch_shapes=[
            pltpu.VMEM(one, bf16),
            pltpu.VMEM(groups, bf16),
            pltpu.VMEM((steps, units, tile), bf16),
            pltpu.VMEM(groups, bf16),
            pltpu.VMEM(groups, bf16),
            pltpu.VMEM((steps, tokens // n, tile), bf16),
            pltpu.SemaphoreType.DMA((steps,)),
            pltpu.SemaphoreType.DMA((steps,)),
            pltpu.SemaphoreType.DMA((steps, 2 * bits)),
            pltpu.SemaphoreType.DMA((steps, 2 * bits)),
        ],
        compiler_params=params(collective_id=0, has_side_effects=True),
    )(own, peer, mask_down, w_down, teacher)
    gh_peer = lax.ppermute(gh_mine, "tensor", [(0, 1), (1, 0)])
    grad_down = pl.pallas_call(
        down_kernel,
        grid=(steps,),
        in_specs=[
            whole((units, tokens)),
            pl.BlockSpec((1, tokens, tile), lambda k: (k, 0, 0)),
            whole(mask_down.shape),
        ],
        out_specs=pl.BlockSpec((units, tile), lambda k: (0, k)),
        out_shape=shape((units, depth), bf16),
        compiler_params=params(),
        cost_estimate=cost(1, 2 * depth * units),
    )(turned, residual, mask_down)
    x_spec, w_spec, _ = specs(tile)
    m_spec = whole(mask_gate.shape)
    wide = (depth // BLOCK, units)
    grad_gate, grad_up = pl.pallas_call(
        weights_kernel,
        grid=(steps,),
        in_specs=[whole(both), whole(one), whole(one), x_spec, m_spec, m_spec],
        out_specs=[w_spec, w_spec],
        out_shape=[shape((depth, units), bf16)] * 2,
        scratch_shapes=[
            pltpu.VMEM((tokens, 2 * units), bf16),
            pltpu.VMEM((2, *wide), f32),
        ],
        compiler_params=params(),
        cost_estimate=cost(2, 4 * depth * units),
    )(factors, gh, gh_peer, hidden_in, mask_gate, mask_up)
    return (grad_gate, grad_up, grad_down)


def on_device(n, tensor, *args):
    tokens, depth = args[0].shape
    units = args[2].shape[1]
    fits = tensor == 2 and n >= 4 and n & (n - 1) == 0 and tokens % (16 * n) == 0
    if fits and depth % (2 * TILE) == 0 and units % 256 == 0:
        return with_kernels(n, *args)
    return plain(*args)


def solution(mesh):
    in_specs = (
        P(None, "tensor"),
        P(None, "tensor"),
        P("tensor", "dp"),
        P("tensor", "dp"),
        P("dp", "tensor"),
        P("tensor", "dp"),
        P("tensor", "dp"),
        P("dp", "tensor"),
    )
    out_specs = (P("tensor", "dp"), P("tensor", "dp"), P("dp", "tensor"))
    return jax.shard_map(
        functools.partial(on_device, mesh.shape["dp"], mesh.shape["tensor"]),
        mesh=mesh,
         in_specs=in_specs, out_specs=out_specs, check_vma=False
    )
```
